32 devices in a mesh: bulk: 8 (over y, x, core), view: 4 (over z).
Axes of the slice: x: 2, y: 2, z: 4, core: 2. Of those that a mesh axis runs over, the one named last changes fastest.
Arguments:
- planes: bfloat16 [32, 512, 512], P('view', 'bulk'), may hold values from -6 to 6
- cand_index: int32 [8, 4, 8, 128], P('bulk', 'view'), may hold values from 0 to 2047
- recv_slot: int32 [8, 4, 8, 128], P('bulk', 'view'), may hold values from 0 to 1023
- recv_count: int32 [8, 4, 8], P('bulk', 'view'), may hold values from 1 to 128, as said below
Outputs:
- dog: bfloat16 [32, 512, 512], P(None, 'bulk', 'view')
- descriptors: float32 [8, 4, 1024, 128], P('bulk', 'view')
The draws below stay inside these ranges and needn't reach their ends.
Inputs may be any that keep to these rules, and one draw needn't show every extreme that they name: `recv_count`: for each owner and view either every brick offers 128 accepted rows, or each brick has 16 to 64 accepted rows (at least 1); some owner and view accepts 128 from every brick.
All inputs are finite; a program needn't handle non-finite values.
Results may differ from the reference program's by a relative error of at most 0.0034.
Values may be sent and summed in bfloat16 or wider, within the bound.
No kernel may reach another device: no remote copies, remote signals or barrier semaphores. Data moves between devices by JAX's collectives and lax.ppermute only.
A program may use at most 64 MiB of HBM per device.

```python
import math
import jax
import jax.numpy as jnp
from jax import lax

NZ = 32
CY = 64
CX = 128
RADIUS = 8
CAND = 128
SLOTS = 1024
NY = 512
NX = 512
N_BULK = 8
N_VIEW = 4


def draw_recv_count(key, part):
    busy_key, level_key, owner_key, view_key = jax.random.split(key, 4)
    busy = jax.random.randint(busy_key, (N_BULK, N_VIEW, 1), 0, 4) == 0
    forced_owner = jax.random.randint(owner_key, (), 0, N_BULK)
    forced_view = jax.random.randint(view_key, (), 0, N_VIEW)
    owner_ids = jnp.arange(N_BULK, dtype=jnp.int32)[:, None, None]
    view_ids = jnp.arange(N_VIEW, dtype=jnp.int32)[None, :, None]
    busy = busy | (owner_ids == forced_owner) & (view_ids == forced_view)
    lowest = max(1, CAND // 8)
    highest = max(lowest, CAND // 2) + 1
    levels = jax.random.randint(level_key, (N_BULK, N_VIEW, N_BULK), lowest, highest)
    return jnp.where(busy, CAND, levels).astype(jnp.int32)


def set_ends(entries, key, low, high):
    place = [jax.random.randint(jax.random.fold_in(key, axis), (), 0, length) for axis, length in enumerate(entries.shape)]
    widest = entries.shape.index(max(entries.shape))
    neighbour = place[:widest] + [(place[widest] + 1) % entries.shape[widest]] + place[widest + 1:]
    return entries.at[tuple(place)].set(low).at[tuple(neighbour)].set(high)


def steps_of(rng, extent, shards, low, top_value):
    def one(dim, shards_of):
        steps = jax.random.uniform(jax.random.fold_in(jax.random.fold_in(rng, 6), dim), (shards_of,), jnp.float32, low / len(shards), top_value / len(shards))
        return jnp.repeat(jnp.exp(steps), extent[dim] // shards_of).reshape((-1,) + (1,) * (len(extent) - dim - 1))

    level = one(*shards[0])
    for cut in shards[1:]:
        level = level * one(*cut)
    return level


def normal_values(stream_key, dims, width, limit, shards=(), held_as=jnp.bfloat16):
    array = width * jax.random.normal(stream_key, dims, jnp.float32)
    if shards:
        array = array * steps_of(stream_key, dims, shards, -0.22, 0.18)
    return jnp.clip(array, -limit, limit).astype(held_as)


def setup_inputs(seed: int = 0) -> dict:
    arg_keys = jax.random.split(jax.random.key(seed), 5)
    planes = normal_values(arg_keys[0], (NZ, NY, NX), 1.0, 6.0, ((0, 4), (1, 8)))
    cand_index = set_ends(jax.random.randint(arg_keys[1], (N_BULK, N_VIEW, N_BULK, CAND), 0, NZ * CY), jax.random.fold_in(arg_keys[1], 1), 0, (NZ * CY) - 1).astype(jnp.int32)
    recv_slot = set_ends(jax.random.randint(arg_keys[2], (N_BULK, N_VIEW, N_BULK, CAND), 0, SLOTS), jax.random.fold_in(arg_keys[2], 1), 0, SLOTS - 1).astype(jnp.int32)
    recv_count = draw_recv_count(jax.random.fold_in(arg_keys[4], 71), 0)
    return {"planes": planes, "cand_index": cand_index, "recv_slot": recv_slot, "recv_count": recv_count}


narrow_sigma = (1.0, 2.0, 2.0)
broad_sigma = (1.6, 3.2, 3.2)
contrast = 20.0
epsilon = 1e-06

def gauss_taps(sigma, radius):
    weights = [math.exp(-0.5 * (offset / sigma) ** 2) for offset in range(-radius, radius + 1)]
    scale_total = sum(weights)
    return [weight / scale_total for weight in weights]

def tap_table(radius):
    return [[gauss_taps(narrow_sigma[along], radius), gauss_taps(broad_sigma[along], radius)] for along in range(3)]

def smooth(fields, weights, along, radius):
    length = fields.shape[along] - 2 * radius
    total = None
    for offset in range(2 * radius + 1):
        shifted = lax.slice_in_dim(fields, offset, offset + length, axis=along).astype(jnp.float32)
        term = weights[:, offset].reshape((2,) + (1,) * (fields.ndim - 1)) * shifted
        total = term if total is None else total + term
    return total

def reference(planes, cand_index, recv_slot, recv_count):
    table = jnp.asarray(tap_table(RADIUS), jnp.float32)
    padded = jnp.pad(planes, ((RADIUS, RADIUS), (RADIUS, RADIUS), (RADIUS, RADIUS)))

    def one_block(block):
        start = (block * CY).astype(jnp.int32)
        window = lax.dynamic_slice_in_dim(padded, start, CY + 2 * RADIUS, axis=1)
        fields = smooth(window[None], table[0], 1, RADIUS)
        fields = smooth(fields, table[1], 2, RADIUS)
        fields = smooth(fields, table[2], 3, RADIUS)
        return (contrast * (fields[0] - fields[1])).astype(jnp.bfloat16)
    blocks = lax.map(one_block, jnp.arange(N_BULK, dtype=jnp.int32))
    dog = jnp.transpose(blocks, (1, 0, 2, 3)).reshape(NZ, NY, NX)
    bricks = dog.reshape(NZ, N_BULK, CY, N_VIEW, CX).transpose(1, 3, 0, 2, 4).reshape(N_BULK, N_VIEW, NZ * CY, CX)

    def take_rows(whole_brick, picks):
        return jnp.take(whole_brick, picks, axis=0)

    def one_view(view_rows, view_slots):
        return jax.ops.segment_sum(view_rows.reshape(-1, CX), view_slots.reshape(-1), num_segments=SLOTS)

    def one_owner(owner):
        index = lax.dynamic_index_in_dim(cand_index, owner, axis=2, keepdims=False)
        rows = jax.vmap(jax.vmap(take_rows))(bricks, index)
        slots = lax.dynamic_index_in_dim(recv_slot, owner, axis=0, keepdims=False)
        counts = lax.dynamic_index_in_dim(recv_count, owner, axis=0, keepdims=False)
        valid = jnp.arange(CAND, dtype=jnp.int32)[None, None, :] < counts[:, :, None]
        rows = jnp.transpose(rows, (1, 0, 2, 3)).astype(jnp.float32) * valid[..., None].astype(jnp.float32)
        summed = jax.vmap(one_view)(rows, slots)
        return summed / jnp.sqrt(lax.optimization_barrier(jnp.mean(summed * summed, axis=-1, keepdims=True)) + epsilon)
    descriptors = lax.map(one_owner, jnp.arange(N_BULK, dtype=jnp.int32))
    return (dog, descriptors)
```

```python
import math

import jax
import jax.numpy as jnp
import numpy as np
from jax import lax
from jax.experimental import pallas as pl
from jax.experimental.pallas import tpu as pltpu
from jax.sharding import PartitionSpec as P

RADIUS = 8
SLOTS = 1024
LANES = 128

narrow_sigma = (1.0, 2.0, 2.0)
broad_sigma = (1.6, 3.2, 3.2)
contrast = 20.0
epsilon = 1e-06

F32 = jnp.float32
BF16 = jnp.bfloat16


def gauss_taps(sigma, radius):
    weights = [math.exp(-0.5 * (offset / sigma) ** 2) for offset in range(-radius, radius + 1)]
    scale_total = sum(weights)
    return [weight / scale_total for weight in weights]


def taps(along):
    return [
        np.asarray(gauss_taps(sigma[along], RADIUS), np.float32)
        for sigma in (narrow_sigma, broad_sigma)
    ]


def split_bf16(array):
    high = array.astype(jnp.bfloat16)
    low = (array - high.astype(np.float32)).astype(jnp.bfloat16)
    return high, low


def band(where_in, where_out, tap):
    offset = np.asarray(where_in)[:, None] - np.asarray(where_out)[None, :] + RADIUS
    inside = (offset >= 0) & (offset <= 2 * RADIUS)
    return np.where(inside, tap[np.clip(offset, 0, 2 * RADIUS)], 0).astype(np.float32)


def x_weights(lane_groups):
    outs = np.arange(LANES)
    margin = list(range(-RADIUS, 0)) + list(range(LANES, LANES + RADIUS))
    both = [
        np.concatenate([band(outs, outs, tap), np.tile(band(margin, outs, tap), (lane_groups, 1))])
        for tap in taps(2)
    ]
    return np.stack(split_bf16(np.concatenate(both, axis=1)))


def y_weights(rows):
    low_edge, high_edge = list(range(RADIUS)), list(range(rows - RADIUS, rows))
    low_halo, high_halo = list(range(-RADIUS, 0)), list(range(rows, rows + RADIUS))
    interior = list(range(RADIUS, rows - RADIUS))
    orders = (
        high_edge + low_edge + high_halo + low_halo + interior,
        low_edge + high_edge + low_halo + high_halo + interior,
    )
    result = []
    for order in orders:
        fields = []
        for tap in taps(1):
            high, low = split_bf16(band(order, np.arange(rows), tap).T)
            wide = np.concatenate([high, low, high], axis=1)
            pad = -wide.shape[1] % LANES
            fields.append(np.pad(wide, ((0, 0), (0, pad))))
        result.append(np.stack(fields))
    return np.stack(result)


def edge_rows(zlocal):
    return -(-(zlocal + 1) * RADIUS // 16) * 16


def pack_kernel(planes_ref, *outs):
    views = len(outs) // 2
    edges, inner = outs[:views], outs[views:]
    zlocal, rows = planes_ref.shape[:2]
    me = lax.axis_index("view")
    odd = lax.axis_index("bulk") % 2 == 1
    lane = lax.broadcasted_iota(jnp.int32, (rows, LANES), 1)
    for k in range(views):
        dest = me ^ k

        def tile(z, which):
            return planes_ref[z, :, pl.ds(pl.multiple_of(which * LANES, LANES), LANES)].astype(F32)

        left = jnp.maximum(dest - 1, 0)
        right = jnp.minimum(dest + 1, views - 1)
        lowest = jnp.where(dest > 0, LANES - RADIUS, LANES)
        highest = jnp.where(dest < views - 1, RADIUS, 0)
        groups = []
        packed = jnp.zeros((rows, LANES), F32)
        for z in range(zlocal):
            margin = jnp.where(
                lane < highest, tile(z, right), jnp.where(lane >= lowest, tile(z, left), 0.0)
            )
            packed = packed + pltpu.roll(margin, (2 * RADIUS * z + RADIUS) % LANES, 1)
            groups.append(tile(z, dest))
        groups.append(packed)
        low = jnp.concatenate([g[:RADIUS] for g in groups], axis=0)
        high = jnp.concatenate([g[rows - RADIUS :] for g in groups], axis=0)
        pad = edges[k].shape[1] - low.shape[0]
        if pad:
            fill = jnp.zeros((pad, LANES), F32)
            low = jnp.concatenate([low, fill], axis=0)
            high = jnp.concatenate([high, fill], axis=0)
        edges[k][0] = jnp.where(odd, low, high).astype(BF16)
        edges[k][1] = jnp.where(odd, high, low).astype(BF16)
        for g, group in enumerate(groups):
            inner[k][g] = group[RADIUS : rows - RADIUS].astype(BF16)


def gather_edges_kernel(*refs):
    views = len(refs) - 2
    for k in range(views):
        for part in range(2):
            refs[views + part][k] = refs[k][part]


def filter_kernel(views, owners, *refs):
    edges = refs[:views]
    inner = refs[views : 2 * views]
    halo = refs[2 * views : 2 * views + 2]
    wx_ref, wy_ref, index_ref = refs[2 * views + 2 : 2 * views + 5]
    dog_ref = refs[2 * views + 5]
    chosen = refs[2 * views + 6 : 2 * views + 6 + owners]
    fields = refs[2 * views + 6 + owners :]
    planes_z, rows = dog_ref.shape[:2]
    zlocal = planes_z // views
    staged_rows = rows + 2 * RADIUS
    me = lax.axis_index("view")
    brick = lax.axis_index("bulk")
    parity = brick % 2

    def pieces(k):
        small = [edges[k][0], edges[k][1], halo[0][k], halo[1][k]]
        return [s.astype(F32) for s in small]

    small = [pieces(k) for k in range(views)]

    def rows_of(k, g):
        top = jnp.concatenate([s[g * RADIUS : (g + 1) * RADIUS] for s in small[k]], axis=0)
        return jnp.concatenate([top.astype(BF16), inner[k][g]], axis=0)

    margins = jnp.concatenate([rows_of(k, zlocal) for k in range(views)], axis=0)
    group = lax.broadcasted_iota(jnp.int32, (LANES, 2 * LANES), 0) // (2 * RADIUS)

    def x_pass(z):
        main = jnp.concatenate([rows_of(k, z) for k in range(views)], axis=0)
        operand = jnp.concatenate([main, margins], axis=1)
        total = None
        for part in range(2):
            margin_w = jnp.where(group == z, wx_ref[part, LANES:].astype(F32), 0.0).astype(BF16)
            weight = jnp.concatenate([wx_ref[part, :LANES], margin_w], axis=0)
            term = jnp.dot(operand, weight, preferred_element_type=F32)
            total = term if total is None else total + term
        return total

    wy = [wy_ref[parity, f] for f in range(2)]
    depth = wy[0].shape[1]
    fill = depth - 3 * staged_rows
    for z in range(0, zlocal, 2):
        pair = [x_pass(z), x_pass(z + 1)]
        for k in range(views):
            at = (me ^ k) * zlocal + z
            for f in range(2):
                data = jnp.concatenate(
                    [
                        p[k * staged_rows : (k + 1) * staged_rows, f * LANES : (f + 1) * LANES]
                        for p in pair
                    ],
                    axis=1,
                )
                high = data.astype(BF16)
                low = (data - high.astype(F32)).astype(BF16)
                parts = [high, high, low]
                if fill:
                    parts.append(jnp.zeros((fill, 2 * LANES), BF16))
                out = jnp.dot(wy[f], jnp.concatenate(parts, axis=0), preferred_element_type=F32)
                fields[f][at] = out[:, :LANES]
                fields[f][at + 1] = out[:, LANES:]

    z_taps = taps(0)
    scale = (contrast, -contrast)
    tile_rows = 16

    def z_pass(step, carry):
        at = pl.ds(pl.multiple_of(step * tile_rows, tile_rows), tile_rows)
        data = [[fields[f][z, at, :] for z in range(planes_z)] for f in range(2)]
        for z in range(planes_z):
            total = None
            for f in range(2):
                for reach in range(RADIUS + 1):
                    weight = float(scale[f] * z_taps[f][RADIUS + reach])
                    sides = [data[f][q] for q in {z - reach, z + reach} if 0 <= q < planes_z]
                    if not sides:
                        continue
                    both = sides[0] if len(sides) == 1 else sides[0] + sides[1]
                    term = weight * both
                    total = term if total is None else total + term
            dog_ref[z, at, :] = total.astype(BF16)
        return carry

    lax.fori_loop(0, rows // tile_rows, z_pass, 0)

    flat = dog_ref[...].reshape(planes_z * rows, LANES)
    wanted = jnp.concatenate(
        [index_ref[pl.ds(brick ^ m, 1), :] for m in range(owners)], axis=0
    ).astype(F32)
    columns = jnp.transpose(wanted)
    offered = columns.shape[0]
    position = lax.broadcasted_iota(jnp.int32, (offered, planes_z * rows), 1).astype(F32)
    for m in range(owners):
        onehot = jnp.where(columns[:, m : m + 1] == position, 1.0, 0.0).astype(BF16)
        chosen[m][...] = jnp.dot(onehot, flat, preferred_element_type=F32).astype(BF16)


def merge_kernel(owners, *refs):
    rows = refs[:owners]
    slot_ref, count_ref, out_ref = refs[owners:]
    owner = lax.axis_index("bulk")
    slots = out_ref.shape[0]
    offered = slot_ref.shape[1]
    candidate = lax.broadcasted_iota(jnp.int32, (1, offered), 1)
    block = 256
    received = jnp.concatenate([r[...] for r in rows], axis=0)
    targets = []
    for m in range(owners):
        slot = slot_ref[pl.ds(owner ^ m, 1), :]
        targets.append(jnp.where(candidate < count_ref[0, owner ^ m], slot, -1))
    target = jnp.concatenate(targets, axis=1)
    for start in range(0, slots, block):
        position = start + lax.broadcasted_iota(jnp.int32, (block, owners * offered), 0)
        onehot = jnp.where(position == target, 1.0, 0.0).astype(BF16)
        summed = jnp.dot(onehot, received, preferred_element_type=F32)
        scale = lax.rsqrt(jnp.mean(summed * summed, axis=-1, keepdims=True) + epsilon)
        out_ref[start : start + block] = summed * scale


def swap(block, axis, distance):
    count = lax.axis_size(axis)
    return lax.ppermute(block, axis, [(i, i ^ distance) for i in range(count)])


def local(planes, cand_index, recv_slot, recv_count):
    views = lax.axis_size("view")
    bricks = lax.axis_size("bulk")
    zlocal, rows, width = planes.shape
    planes_z = zlocal * views
    owners, offered = cand_index.shape[2:]
    vmem = pl.BlockSpec(memory_space=pltpu.VMEM)
    smem = pl.BlockSpec(memory_space=pltpu.SMEM)
    params = pltpu.CompilerParams(vmem_limit_bytes=48 * 1024 * 1024)
    edge = jax.ShapeDtypeStruct((2, edge_rows(zlocal), LANES), BF16)
    body = jax.ShapeDtypeStruct((zlocal + 1, rows - 2 * RADIUS, LANES), BF16)
    halo = jax.ShapeDtypeStruct((views, edge_rows(zlocal), LANES), BF16)

    packed = pl.pallas_call(
        pack_kernel,
        out_shape=[edge] * views + [body] * views,
        in_specs=[vmem],
        out_specs=[vmem] * (2 * views),
        compiler_params=params,
    )(planes)
    edges = [packed[0]] + [swap(packed[k], "view", k) for k in range(views - 1, 0, -1)][::-1]
    inner = [packed[views]] + [
        swap(packed[views + k], "view", k) for k in range(views - 1, 0, -1)
    ][::-1]
    near, far = pl.pallas_call(
        gather_edges_kernel,
        out_shape=[halo] * 2,
        in_specs=[vmem] * views,
        out_specs=[vmem] * 2,
        compiler_params=params,
    )(*edges)
    far_pairs = [(i, i + 1) for i in range(1, bricks - 1, 2)]
    far_pairs = far_pairs + [(target, source) for source, target in far_pairs]
    near = swap(near, "bulk", 1)
    far = lax.ppermute(far, "bulk", far_pairs)

    dog, *chosen = pl.pallas_call(
        lambda *refs: filter_kernel(views, owners, *refs),
        out_shape=[jax.ShapeDtypeStruct((planes_z, rows, LANES), BF16)]
        + [jax.ShapeDtypeStruct((offered, LANES), BF16)] * owners,
        in_specs=[vmem] * (2 * views + 5),
        out_specs=[vmem] * (1 + owners),
        scratch_shapes=[pltpu.VMEM((planes_z, rows, LANES), F32)] * 2,
        compiler_params=params,
    )(
        *edges,
        *inner,
        near,
        far,
        jnp.asarray(x_weights(LANES // (2 * RADIUS))),
        jnp.asarray(y_weights(rows)),
        cand_index.reshape(owners, offered),
    )
    received = [chosen[0]] + [
        swap(chosen[m], "bulk", m) for m in range(owners - 1, 0, -1)
    ][::-1]
    descriptors = pl.pallas_call(
        lambda *refs: merge_kernel(owners, *refs),
        out_shape=jax.ShapeDtypeStruct((SLOTS, LANES), F32),
        in_specs=[vmem] * (owners + 1) + [smem],
        out_specs=vmem,
        compiler_params=params,
    )(*received, recv_slot.reshape(owners, offered), recv_count.reshape(1, owners))
    return (dog, descriptors.reshape(1, 1, SLOTS, LANES))


def solution(mesh):
    in_specs = (
        P("view", "bulk", None),
        P("bulk", "view", None, None),
        P("bulk", "view", None, None),
        P("bulk", "view", None),
    )
    out_specs = (P(None, "bulk", "view"), P("bulk", "view", None, None))
    return jax.shard_map(local, mesh=mesh, in_specs=in_specs, out_specs=out_specs, check_vma=False)
```

```python
import math

import jax
import jax.numpy as jnp
import numpy as np
from jax import lax
from jax.experimental import pallas as pl
from jax.experimental.pallas import tpu as pltpu
from jax.sharding import PartitionSpec as P

RADIUS = 8
SLOTS = 1024
LANES = 128
BLOCK = 256
TILE = 16

narrow_sigma = (1.0, 2.0, 2.0)
broad_sigma = (1.6, 3.2, 3.2)
contrast = 20.0
epsilon = 1e-06

F32 = jnp.float32
BF16 = jnp.bfloat16


def gauss_taps(sigma, radius):
    weights = [math.exp(-0.5 * (offset / sigma) ** 2) for offset in range(-radius, radius + 1)]
    scale_total = sum(weights)
    return [weight / scale_total for weight in weights]


def taps(along):
    return [
        np.asarray(gauss_taps(sigma[along], RADIUS), np.float32)
        for sigma in (narrow_sigma, broad_sigma)
    ]


def split_bf16(array):
    high = array.astype(jnp.bfloat16)
    low = (array - high.astype(np.float32)).astype(jnp.bfloat16)
    return high, low


def band(where_in, where_out, tap):
    offset = np.asarray(where_in)[:, None] - np.asarray(where_out)[None, :] + RADIUS
    inside = (offset >= 0) & (offset <= 2 * RADIUS)
    return np.where(inside, tap[np.clip(offset, 0, 2 * RADIUS)], 0).astype(np.float32)


def x_weights():
    outs = np.arange(LANES)
    margin = list(range(-RADIUS, 0)) + list(range(LANES, LANES + RADIUS))
    main = np.concatenate([band(outs, outs, tap) for tap in taps(2)], axis=1)
    edge = np.concatenate([band(margin, outs, tap) for tap in taps(2)], axis=1)
    edge = np.tile(edge, (LANES // (2 * RADIUS), 1))
    return (
        np.concatenate(split_bf16(main), axis=0),
        np.concatenate(split_bf16(edge), axis=0),
    )


def y_weights(rows):
    low_edge, high_edge = list(range(RADIUS)), list(range(rows - RADIUS, rows))
    interior = list(range(RADIUS, rows - RADIUS))
    return np.stack(
        [
            np.stack(
                [
                    np.concatenate(
                        split_bf16(band(edges + interior, np.arange(rows), tap).T) * 2, axis=1
                    )
                    for tap in taps(1)
                ]
            )
            for edges in (high_edge + low_edge, low_edge + high_edge)
        ]
    )


def y_margin_weights(rows, pairs):
    low_halo, high_halo = list(range(-RADIUS, 0)), list(range(rows, rows + RADIUS))
    outs = list(range(RADIUS)) + list(range(rows - RADIUS, rows))
    result = []
    for order in (high_halo + low_halo, low_halo + high_halo):
        wide = [
            np.concatenate(split_bf16(band(order, outs, tap).T) * 2, axis=1).astype(np.float32)
            for tap in taps(1)
        ]
        result.append(np.stack([np.kron(np.eye(pairs, dtype=np.float32), w) for w in wide]))
    return np.stack(result).astype(jnp.bfloat16)


def edge_rows(zlocal):
    return -(-(zlocal + 1) * RADIUS // 16) * 16


def column_tile(source, which):
    at = pl.ds(pl.multiple_of(which * LANES, LANES), LANES)
    return source(at)


def with_margin(source, dest, views, rows):
    lane = lax.broadcasted_iota(jnp.int32, (rows, LANES), 1)
    left = column_tile(source, jnp.maximum(dest - 1, 0))
    right = column_tile(source, jnp.minimum(dest + 1, views - 1))
    lowest = jnp.where(dest > 0, LANES - RADIUS, LANES)
    highest = jnp.where(dest < views - 1, RADIUS, 0)
    margin = jnp.where(lane < highest, right, jnp.where(lane >= lowest, left, 0.0))
    return column_tile(source, dest), margin


def place_margin(margin, z):
    return pltpu.roll(margin, (2 * RADIUS * z + RADIUS) % LANES, 1)


def pack_kernel(shifts, planes_ref, *outs):
    views = len(shifts)
    edges, inner = outs[:views], outs[views:]
    zlocal, rows = planes_ref.shape[:2]
    me = lax.axis_index("view")
    odd = lax.axis_index("bulk") % 2 == 1
    for k, shift in enumerate(shifts):
        groups = []
        packed = None
        for z in range(zlocal):
            main, margin = with_margin(
                lambda at: planes_ref[z, :, at].astype(F32), me ^ shift, views, rows
            )
            groups.append(main)
            placed = place_margin(margin, z)
            packed = placed if packed is None else packed + placed
        groups.append(packed)
        low = [g[:RADIUS] for g in groups]
        high = [g[rows - RADIUS :] for g in groups]
        pad = edges[k].shape[1] - len(groups) * RADIUS
        if pad:
            low.append(jnp.zeros((pad, LANES), F32))
            high.append(jnp.zeros((pad, LANES), F32))
        low, high = jnp.concatenate(low, axis=0), jnp.concatenate(high, axis=0)
        edges[k][0] = jnp.where(odd, low, high).astype(BF16)
        edges[k][1] = jnp.where(odd, high, low).astype(BF16)
        for g, group in enumerate(groups):
            inner[k][g] = group[RADIUS : rows - RADIUS].astype(BF16)


def margin_kernel(passed_ref, *refs):
    *edges, near_ref, far_ref, _ = refs
    del passed_ref
    for k, edge in enumerate(edges):
        near_ref[k] = edge[0]
        far_ref[k] = edge[1]


def prepare_kernel(chips, main_ref, side_ref, wy_ref, wr_ref, index_ref, slot_ref, count_ref, *outs):
    wm_ref, ws_ref, inside_ref, margin_ref, column_ref, target_ref = outs
    brick = lax.axis_index("bulk")
    wm_ref[...] = main_ref[...]
    inside_ref[...] = wy_ref[brick % 2]
    group = lax.broadcasted_iota(jnp.int32, side_ref.shape, 0) % LANES // (2 * RADIUS)
    for z in range(ws_ref.shape[0]):
        ws_ref[z] = jnp.where(group == z, side_ref[...].astype(F32), 0.0).astype(BF16)
    margin_ref[...] = wr_ref[brick % 2]
    wanted = jnp.concatenate(
        [index_ref[pl.ds(brick ^ c ^ core, 1), :] for c in chips for core in range(2)], axis=0
    )
    column_ref[...] = jnp.transpose(wanted.astype(F32))
    candidate = lax.broadcasted_iota(jnp.int32, slot_ref.shape, 1)
    target = jnp.where(candidate < count_ref[...], slot_ref[...], -1)
    target_ref[...] = target


def twice(block):
    return jnp.concatenate([block, block], axis=1)


def split_stack(data):
    high = data.astype(BF16)
    low = (data - high.astype(F32)).astype(BF16)
    return [high, high, low, low]


def z_pass(load, planes_z):
    data = [[load(f, z) for z in range(planes_z)] for f in range(2)]
    z_taps = taps(0)
    scale = (contrast, -contrast)
    out = []
    for z in range(planes_z):
        total = None
        for f in range(2):
            for reach in range(RADIUS + 1):
                weight = float(scale[f] * z_taps[f][RADIUS + reach])
                near = [z] if reach == 0 else [z - reach, z + reach]
                sides = [data[f][q] for q in near if 0 <= q < planes_z]
                if not sides:
                    continue
                both = sides[0] if len(sides) == 1 else sides[0] + sides[1]
                term = weight * both
                total = term if total is None else total + term
        out.append(total)
    return out


def inner_kernel(shifts, *refs):
    views = len(shifts)
    edges, inner = refs[:views], refs[views : 2 * views]
    wm_ref, ws_ref, wy_ref, dog_ref, edge_ref, *fields = refs[2 * views :]
    zlocal, rows = inner[0].shape[0] - 1, wy_ref.shape[1]
    planes_z = zlocal * views
    me = lax.axis_index("view")

    small = [[edges[k][part].astype(F32) for part in range(2)] for k in range(views)]

    def rows_of(k, g):
        top = [s[g * RADIUS : (g + 1) * RADIUS] for s in small[k]]
        return [jnp.concatenate(top, axis=0).astype(BF16), inner[k][g]]

    def stacked(z):
        return twice(jnp.concatenate([p for k in range(views) for p in rows_of(k, z)], axis=0))

    margins = stacked(zlocal)

    def x_pass(z):
        main = jnp.dot(stacked(z), wm_ref[...], preferred_element_type=F32)
        return main + jnp.dot(margins, ws_ref[z], preferred_element_type=F32)

    for z in range(0, zlocal, 2):
        pair = [x_pass(z), x_pass(z + 1)]
        for k in range(views):
            at = (me ^ shifts[k]) * zlocal + z
            for f in range(2):
                data = jnp.concatenate(
                    [
                        p[k * rows : (k + 1) * rows, f * LANES : (f + 1) * LANES]
                        for p in pair
                    ],
                    axis=1,
                )
                operand = jnp.concatenate(split_stack(data), axis=0)
                out = jnp.dot(wy_ref[f], operand, preferred_element_type=F32)
                fields[f][at] = out[:, :LANES]
                fields[f][at + 1] = out[:, LANES:]

    def tile(step, carry):
        start = step * TILE + RADIUS
        at = pl.ds(pl.multiple_of(start, RADIUS), TILE)
        to = pl.ds(pl.multiple_of(step * TILE, TILE), TILE)
        done = z_pass(lambda f, z: fields[f][z, at, :], planes_z)
        for z in range(planes_z):
            dog_ref[z, to, :] = done[z]
        return carry

    lax.fori_loop(0, (rows - 2 * RADIUS) // TILE, tile, 0)
    for f in range(2):
        edge_ref[f, :, :RADIUS] = fields[f][:, :RADIUS]
        edge_ref[f, :, RADIUS:] = fields[f][:, rows - RADIUS :]


def outer_kernel(shifts, chips, *refs):
    views = len(shifts)
    halo, refs = refs[:2], refs[2:]
    inner_ref, edge_ref, wm_ref, ws_ref, wy_ref, column_ref, dog_hbm = refs[:7]
    chosen = refs[7 : 7 + len(chips)]
    fields, dog_ref, written = refs[7 + len(chips) :]
    planes_z, rows = dog_ref.shape[:2]
    zlocal = planes_z // views
    both = 2 * RADIUS
    me = lax.axis_index("view")
    brick = lax.axis_index("bulk")
    ends = (brick == 0) | (brick == lax.axis_size("bulk") - 1)

    def margin(part, k):
        data = halo[part][k].astype(F32)
        return jnp.where(ends, 0.0, data) if part == 1 else data

    small = [[margin(part, k) for part in range(2)] for k in range(views)]

    def rows_of(k, g):
        return [s[g * RADIUS : (g + 1) * RADIUS] for s in small[k]]

    main = [p for k in range(views) for z in range(zlocal) for p in rows_of(k, z)]
    side = [p for k in range(views) for p in rows_of(k, zlocal)]
    main = twice(jnp.concatenate(main, axis=0).astype(BF16))
    side = twice(jnp.concatenate(side, axis=0).astype(BF16))
    main = jnp.dot(main, wm_ref[...], preferred_element_type=F32)
    side = [jnp.dot(side, ws_ref[z], preferred_element_type=F32) for z in range(zlocal)]
    for k in range(views):
        smooth = [
            main[(k * zlocal + z) * both : (k * zlocal + z + 1) * both]
            + side[z][k * both : (k + 1) * both]
            for z in range(zlocal)
        ]
        at = (me ^ shifts[k]) * zlocal
        for f in range(2):
            parts = []
            for z in range(0, zlocal, 2):
                parts += split_stack(
                    jnp.concatenate(
                        [p[:, f * LANES : (f + 1) * LANES] for p in smooth[z : z + 2]], axis=1
                    )
                )
            operand = jnp.concatenate(parts, axis=0)
            out = jnp.dot(wy_ref[f], operand, preferred_element_type=F32)
            for z in range(zlocal):
                row, lane = z // 2 * both, z % 2 * LANES
                fields[f, at + z] = (
                    edge_ref[f, at + z] + out[row : row + both, lane : lane + LANES]
                )

    done = z_pass(lambda f, z: fields[f, z], planes_z)
    for z in range(planes_z):
        whole = [done[z][:RADIUS], inner_ref[z], done[z][RADIUS:]]
        dog_ref[z] = jnp.concatenate(whole, axis=0).astype(BF16)

    parts = written.shape[0]
    copies = []
    for part in range(parts):
        span = pl.ds(part * (planes_z // parts), planes_z // parts)
        copies.append(
            pltpu.make_async_copy(dog_ref.at[span], dog_hbm.at[span], written.at[part])
        )
        copies[-1].start()

    half = planes_z * rows // 2
    flat = dog_ref[...].reshape(2 * half, LANES)
    flat = jnp.concatenate([flat[:half], flat[half:]], axis=1)
    columns = column_ref[...]
    offered = columns.shape[0]
    lane = lax.broadcasted_iota(jnp.int32, (offered, BLOCK), 1).astype(F32).astype(BF16)
    for m in range(2 * len(chips)):
        column = columns[:, m : m + 1]
        later = column >= half
        column = jnp.where(later, column - half, column)
        upper = jnp.floor(column * (1.0 / BLOCK))
        lower = column - BLOCK * upper
        onehot = []
        for j in range(half // BLOCK):
            here = jnp.where(upper == j, lower, -1.0).astype(BF16)
            onehot.append(jnp.where(lane == here, 1.0, 0.0).astype(BF16))
        onehot = jnp.concatenate(onehot, axis=1)
        picked = jnp.dot(onehot, flat, preferred_element_type=F32)
        picked = jnp.where(later, picked[:, LANES:], picked[:, :LANES])
        chosen[m // 2][m % 2] = picked.astype(BF16)
    for copy in copies:
        copy.wait()


def forward_kernel(*refs):
    *rows, out_ref = refs
    for c, row in enumerate(rows):
        out_ref[c] = row[1]


def merge_kernel(chips, *refs):
    rows = refs[: len(chips)]
    passed_ref, target_ref, out_hbm, out_ref, written = refs[len(chips) :]
    owners, offered = target_ref.shape
    slots = out_ref.shape[0]
    owner = lax.axis_index("bulk")
    copies = []
    received = jnp.concatenate(
        [r[0] for r in rows] + [passed_ref[c] for c in range(len(chips))], axis=0
    )
    target = jnp.concatenate(
        [target_ref[pl.ds(owner ^ c ^ core, 1), :] for core in range(2) for c in chips], axis=1
    )
    upper, lower = target >> 8, (target & (BLOCK - 1)).astype(F32)
    place = lax.broadcasted_iota(jnp.int32, (BLOCK, owners * offered), 0).astype(F32).astype(BF16)
    for block in range(slots // BLOCK):
        wanted = jnp.where(upper == block, lower, -1.0).astype(BF16)
        onehot = jnp.where(place == wanted, 1.0, 0.0).astype(BF16)
        summed = jnp.dot(onehot, received, preferred_element_type=F32)
        scale = lax.rsqrt(jnp.mean(summed * summed, axis=-1, keepdims=True) + epsilon)
        span = pl.ds(block * BLOCK, BLOCK)
        out_ref[span] = summed * scale
        copies.append(
            pltpu.make_async_copy(out_ref.at[span], out_hbm.at[span], written.at[block])
        )
        copies[-1].start()
    for copy in copies:
        copy.wait()


def swap(block, axis, distance):
    if distance == 0:
        return block
    count = lax.axis_size(axis)
    return lax.ppermute(block, axis, [(i, i ^ distance) for i in range(count)])


def local(planes, cand_index, recv_slot, recv_count):
    views = lax.axis_size("view")
    bricks = lax.axis_size("bulk")
    zlocal, rows, width = planes.shape
    planes_z = zlocal * views
    owners, offered = cand_index.shape[2:]
    vmem = pl.BlockSpec(memory_space=pltpu.VMEM)
    hbm = pl.BlockSpec(memory_space=pltpu.HBM)
    params = pltpu.CompilerParams(vmem_limit_bytes=48 * 1024 * 1024)
    edge = jax.ShapeDtypeStruct((2, edge_rows(zlocal), LANES), BF16)
    body = jax.ShapeDtypeStruct((zlocal + 1, rows - 2 * RADIUS, LANES), BF16)
    halo = jax.ShapeDtypeStruct((views, edge_rows(zlocal), LANES), BF16)
    targets = jax.ShapeDtypeStruct((owners, offered), jnp.int32)
    shifts = list(range(views - 1, -1, -1))
    chips = list(range(owners - 2, -1, -2))

    packed = pl.pallas_call(
        lambda *refs: pack_kernel(shifts, *refs),
        out_shape=[edge] * views + [body] * views,
        in_specs=[vmem],
        out_specs=[vmem] * (2 * views),
        compiler_params=params,
    )(planes)
    edges = [swap(e, "view", k) for e, k in zip(packed[:views], shifts)]
    inner = [swap(e, "view", k) for e, k in zip(packed[views:], shifts)]

    weights = [*x_weights(), y_weights(rows), y_margin_weights(rows, zlocal // 2)]
    main_w, side_w, inside_w, margin_w, columns, target = pl.pallas_call(
        lambda *refs: prepare_kernel(chips, *refs),
        out_shape=[
            jax.ShapeDtypeStruct(weights[0].shape, BF16),
            jax.ShapeDtypeStruct((zlocal,) + weights[1].shape, BF16),
            jax.ShapeDtypeStruct(weights[2].shape[1:], BF16),
            jax.ShapeDtypeStruct(weights[3].shape[1:], BF16),
            jax.ShapeDtypeStruct((offered, owners), F32),
            targets,
        ],
        in_specs=[vmem] * 7,
        out_specs=[vmem] * 6,
        compiler_params=params,
    )(
        *[jnp.asarray(w) for w in weights],
        cand_index.reshape(owners, offered),
        recv_slot.reshape(owners, offered),
        recv_count.reshape(owners, 1),
    )
    near, far, target = pl.pallas_call(
        margin_kernel,
        out_shape=[halo] * 2 + [targets],
        in_specs=[vmem] * (views + 1),
        out_specs=[vmem] * 3,
        input_output_aliases={0: 2},
        compiler_params=params,
    )(target, *edges)
    far_pairs = [(i, i + 1) for i in range(1, bricks - 1, 2)] + [(0, bricks - 1)]
    far_pairs = far_pairs + [(target, source) for source, target in far_pairs]
    far = lax.ppermute(far, "bulk", far_pairs)
    near = swap(near, "bulk", 1)

    dog, sides = pl.pallas_call(
        lambda *refs: inner_kernel(shifts, *refs),
        out_shape=[
            jax.ShapeDtypeStruct((planes_z, rows - 2 * RADIUS, LANES), F32),
            jax.ShapeDtypeStruct((2, planes_z, 2 * RADIUS, LANES), F32),
        ],
        in_specs=[vmem] * (2 * views + 3),
        out_specs=[vmem] * 2,
        scratch_shapes=[pltpu.VMEM((planes_z, rows, LANES), F32)] * 2,
        compiler_params=params,
    )(*edges, *inner, main_w, side_w, inside_w)

    offers = jax.ShapeDtypeStruct((2, offered, LANES), BF16)
    dog, *chosen = pl.pallas_call(
        lambda *refs: outer_kernel(shifts, chips, *refs),
        out_shape=[jax.ShapeDtypeStruct((planes_z, rows, LANES), BF16)] + [offers] * len(chips),
        in_specs=[vmem] * 8,
        out_specs=[hbm] + [vmem] * len(chips),
        scratch_shapes=[
            pltpu.VMEM((2, planes_z, 2 * RADIUS, LANES), F32),
            pltpu.VMEM((planes_z, rows, LANES), BF16),
            pltpu.SemaphoreType.DMA((8,)),
        ],
        compiler_params=params,
    )(
        near,
        far,
        dog,
        sides,
        main_w,
        side_w,
        margin_w,
        columns,
    )
    received = [swap(c, "bulk", k) for c, k in zip(chosen, chips)]
    passed = pl.pallas_call(
        forward_kernel,
        out_shape=jax.ShapeDtypeStruct((len(chips), offered, LANES), BF16),
        in_specs=[vmem] * len(chips),
        out_specs=vmem,
        compiler_params=params,
    )(*received)
    passed = swap(passed, "bulk", 1)
    descriptors = pl.pallas_call(
        lambda *refs: merge_kernel(chips, *refs),
        out_shape=jax.ShapeDtypeStruct((SLOTS, LANES), F32),
        in_specs=[vmem] * (len(chips) + 2),
        out_specs=hbm,
        scratch_shapes=[
            pltpu.VMEM((SLOTS, LANES), F32),
            pltpu.SemaphoreType.DMA((SLOTS // BLOCK,)),
        ],
        compiler_params=params,
    )(*received, passed, target)
    return (dog, descriptors.reshape(1, 1, SLOTS, LANES))


def solution(mesh):
    in_specs = (
        P("view", "bulk", None),
        P("bulk", "view", None, None),
        P("bulk", "view", None, None),
        P("bulk", "view", None),
    )
    out_specs = (P(None, "bulk", "view"), P("bulk", "view", None, None))
    return jax.shard_map(local, mesh=mesh, in_specs=in_specs, out_specs=out_specs, check_vma=False)
```

```python
import math

import jax
import jax.numpy as jnp
import numpy as np
from jax import lax
from jax.experimental import pallas as pl
from jax.experimental.pallas import tpu as pltpu
from jax.sharding import PartitionSpec as P

RADIUS = 8
SLOTS = 1024
LANES = 128
BLOCK = 256
TILE = 16

narrow_sigma = (1.0, 2.0, 2.0)
broad_sigma = (1.6, 3.2, 3.2)
contrast = 20.0
epsilon = 1e-06

F32 = jnp.float32
BF16 = jnp.bfloat16


def gauss_taps(sigma, radius):
    weights = [math.exp(-0.5 * (offset / sigma) ** 2) for offset in range(-radius, radius + 1)]
    scale_total = sum(weights)
    return [weight / scale_total for weight in weights]


def taps(along):
    return [
        np.asarray(gauss_taps(sigma[along], RADIUS), np.float32)
        for sigma in (narrow_sigma, broad_sigma)
    ]


def stencil(distance, tap):
    total = jnp.zeros(distance.shape, F32)
    for reach in range(RADIUS + 1):
        total = jnp.where(jnp.abs(distance) == reach, float(tap[RADIUS + reach]), total)
    return total


def split(weight):
    high = weight.astype(BF16).astype(F32)
    return high, (weight - high).astype(BF16).astype(F32)


def grid(rows, columns):
    shape = (rows, columns)
    return [lax.broadcasted_iota(jnp.int32, shape, axis) for axis in range(2)]


def x_weights(wm_ref, ws_ref):
    row, column = grid(LANES, LANES)
    place = row % (2 * RADIUS)
    margin = jnp.where(place < RADIUS, place - RADIUS, place - RADIUS + LANES)
    group = lax.broadcasted_iota(jnp.int32, (LANES, 2 * LANES), 0) // (2 * RADIUS)
    for ref, at in ((wm_ref, row), (ws_ref, margin)):
        whole = jnp.concatenate([stencil(at - column, tap) for tap in taps(2)], axis=1)
        for part, value in enumerate(split(whole)):
            span = slice(part * LANES, (part + 1) * LANES)
            if ref is wm_ref:
                ref[span] = value.astype(BF16)
                continue
            for z in range(ref.shape[0]):
                ref[z, span] = jnp.where(group == z, value, 0.0).astype(BF16)


def y_weights(odd, out_ref):
    rows = out_ref.shape[1]
    out, lane = grid(rows, 4 * rows)
    place, block = lane % rows, lane // rows
    first = jnp.where(odd, place, place + rows - RADIUS)
    second = jnp.where(odd, place + rows - 2 * RADIUS, place - RADIUS)
    at = jnp.where(place < RADIUS, first, jnp.where(place < 2 * RADIUS, second, place - RADIUS))
    for f, tap in enumerate(taps(1)):
        high, low = split(stencil(at - out, tap))
        out_ref[f] = jnp.where(block % 2 == 0, high, low).astype(BF16)


def y_margin_weights(odd, rows, out_ref):
    both = 2 * RADIUS
    row, lane = grid(*out_ref.shape[1:])
    out = row % both
    out = jnp.where(out < RADIUS, out, out + rows - both)
    block, place = lane % (4 * both) // both, lane % both
    low, high = place % RADIUS - RADIUS, place % RADIUS + rows
    near = place < RADIUS
    at = jnp.where(jnp.logical_xor(near, odd), high, low)
    same = row // both == lane // (4 * both)
    for f, tap in enumerate(taps(1)):
        top, rest = split(stencil(at - out, tap))
        value = jnp.where(block % 2 == 0, top, rest)
        out_ref[f] = jnp.where(same, value, 0.0).astype(BF16)


def edge_rows(zlocal):
    return -(-(zlocal + 1) * RADIUS // 16) * 16


def column_tile(source, which):
    at = pl.ds(pl.multiple_of(which * LANES, LANES), LANES)
    return source(at)


def with_margin(source, dest, views, rows):
    lane = lax.broadcasted_iota(jnp.int32, (rows, LANES), 1)
    left = column_tile(source, jnp.maximum(dest - 1, 0))
    right = column_tile(source, jnp.minimum(dest + 1, views - 1))
    lowest = jnp.where(dest > 0, LANES - RADIUS, LANES)
    highest = jnp.where(dest < views - 1, RADIUS, 0)
    margin = jnp.where(lane < highest, right, jnp.where(lane >= lowest, left, 0.0))
    return column_tile(source, dest), margin


def place_margin(margin, z):
    return pltpu.roll(margin, (2 * RADIUS * z + RADIUS) % LANES, 1)


def pack_kernel(shifts, planes_ref, *outs):
    views = len(shifts)
    edges, inner = outs[:views], outs[views:]
    zlocal, rows = planes_ref.shape[:2]
    me = lax.axis_index("view")
    odd = lax.axis_index("bulk") % 2 == 1
    for k, shift in enumerate(shifts):
        groups = []
        packed = None
        for z in range(zlocal):
            main, margin = with_margin(
                lambda at: planes_ref[z, :, at].astype(F32), me ^ shift, views, rows
            )
            groups.append(main)
            placed = place_margin(margin, z)
            packed = placed if packed is None else packed + placed
        groups.append(packed)
        low = [g[:RADIUS] for g in groups]
        high = [g[rows - RADIUS :] for g in groups]
        pad = edges[k].shape[1] - len(groups) * RADIUS
        if pad:
            low.append(jnp.zeros((pad, LANES), F32))
            high.append(jnp.zeros((pad, LANES), F32))
        low, high = jnp.concatenate(low, axis=0), jnp.concatenate(high, axis=0)
        edges[k][0] = jnp.where(odd, low, high).astype(BF16)
        edges[k][1] = jnp.where(odd, high, low).astype(BF16)
        for g, group in enumerate(groups):
            inner[k][g] = group[RADIUS : rows - RADIUS].astype(BF16)


def margin_kernel(*refs):
    *edges, near_ref, far_ref, token_ref = refs
    token_ref[...] = jnp.zeros(token_ref.shape, F32)
    for k, edge in enumerate(edges):
        near_ref[k] = edge[0]
        far_ref[k] = edge[1]


def partner(brick, chip, core):
    return brick ^ jnp.where(brick % 2 == 1, chip[1], chip[0]) ^ core


def prepare_kernel(packed_ref, wm_ref, ws_ref, inside_ref, margin_ref):
    del packed_ref
    odd = lax.axis_index("bulk") % 2 == 1
    x_weights(wm_ref, ws_ref)
    y_weights(odd, inside_ref)
    y_margin_weights(odd, inside_ref.shape[1], margin_ref)


def lists_kernel(chips, token_ref, index_ref, slot_ref, count_ref, column_ref, target_ref):
    del token_ref
    brick = lax.axis_index("bulk")
    wanted = jnp.concatenate(
        [index_ref[pl.ds(partner(brick, c, core), 1), :] for c in chips for core in range(2)],
        axis=0,
    )
    column_ref[...] = jnp.transpose(wanted.astype(F32))
    candidate = lax.broadcasted_iota(jnp.int32, slot_ref.shape, 1)
    counts = jnp.broadcast_to(count_ref[...].astype(F32), (LANES, count_ref.shape[1]))
    counts = jnp.transpose(counts)[:, : slot_ref.shape[1]].astype(jnp.int32)
    target_ref[...] = jnp.where(candidate < counts, slot_ref[...], -1)


def twice(block):
    return jnp.concatenate([block, block], axis=1)


def split_stack(data):
    high = data.astype(BF16)
    low = (data - high.astype(F32)).astype(BF16)
    return [high, high, low, low]


def z_pass(load, planes_z):
    data = [[load(f, z) for z in range(planes_z)] for f in range(2)]
    z_taps = taps(0)
    scale = (contrast, -contrast)
    out = []
    for z in range(planes_z):
        total = None
        for f in range(2):
            for reach in range(RADIUS + 1):
                weight = float(scale[f] * z_taps[f][RADIUS + reach])
                near = [z] if reach == 0 else [z - reach, z + reach]
                sides = [data[f][q] for q in near if 0 <= q < planes_z]
                if not sides:
                    continue
                both = sides[0] if len(sides) == 1 else sides[0] + sides[1]
                term = weight * both
                total = term if total is None else total + term
        out.append(total)
    return out


def plane_passes(edges, inner, wm_ref, ws_ref, wy_ref, write):
    count = len(edges)
    zlocal, rows = inner[0].shape[0] - 1, wy_ref.shape[1]
    small = [[e[part].astype(F32) for part in range(2)] for e in edges]

    def rows_of(k, g):
        top = [s[g * RADIUS : (g + 1) * RADIUS] for s in small[k]]
        return [jnp.concatenate(top, axis=0).astype(BF16), inner[k][g]]

    def stacked(z):
        return twice(jnp.concatenate([p for k in range(count) for p in rows_of(k, z)], axis=0))

    margins = stacked(zlocal)

    def x_pass(z):
        main = jnp.dot(stacked(z), wm_ref[...], preferred_element_type=F32)
        return main + jnp.dot(margins, ws_ref[z], preferred_element_type=F32)

    for z in range(0, zlocal, 2):
        pair = [x_pass(z), x_pass(z + 1)]
        for k in range(count):
            for f in range(2):
                data = jnp.concatenate(
                    [
                        p[k * rows : (k + 1) * rows, f * LANES : (f + 1) * LANES]
                        for p in pair
                    ],
                    axis=1,
                )
                operand = jnp.concatenate(split_stack(data), axis=0)
                out = jnp.dot(wy_ref[f], operand, preferred_element_type=F32)
                write(k, z, f, out[:, :LANES])
                write(k, z + 1, f, out[:, LANES:])


def early_kernel(token_ref, edge_ref, inner_ref, wm_ref, ws_ref, wy_ref, out_ref, _):
    del token_ref

    def write(k, z, f, value):
        del k
        out_ref[f, z] = value

    plane_passes([edge_ref], [inner_ref], wm_ref, ws_ref, wy_ref, write)


def late_kernel(shifts, target_ref, own_ref, *refs):
    del target_ref
    *refs, wm_ref, ws_ref, wy_ref, fields, _ = refs
    count = len(refs) // 2
    zlocal = own_ref.shape[1]
    me = lax.axis_index("view")
    for f in range(2):
        fields[f, pl.ds(me * zlocal, zlocal)] = own_ref[f]

    def write(k, z, f, value):
        fields[f, (me ^ shifts[k]) * zlocal + z] = value

    plane_passes(refs[:count], refs[count:], wm_ref, ws_ref, wy_ref, write)


def border_kernel(shifts, target_ref, near_ref, far_ref, wm_ref, ws_ref, wy_ref, out_ref, _):
    del target_ref
    views = len(shifts)
    halo = (near_ref, far_ref)
    zlocal = out_ref.shape[1] // views
    both = 2 * RADIUS
    me = lax.axis_index("view")
    brick = lax.axis_index("bulk")
    ends = (brick == 0) | (brick == lax.axis_size("bulk") - 1)

    def margin(part, k):
        data = halo[part][k].astype(F32)
        return jnp.where(ends, 0.0, data) if part == 1 else data

    small = [[margin(part, k) for part in range(2)] for k in range(views)]

    def rows_of(k, g):
        return [s[g * RADIUS : (g + 1) * RADIUS] for s in small[k]]

    main = [p for k in range(views) for z in range(zlocal) for p in rows_of(k, z)]
    side = [p for k in range(views) for p in rows_of(k, zlocal)]
    main = twice(jnp.concatenate(main, axis=0).astype(BF16))
    side = twice(jnp.concatenate(side, axis=0).astype(BF16))
    main = jnp.dot(main, wm_ref[...], preferred_element_type=F32)
    side = [jnp.dot(side, ws_ref[z], preferred_element_type=F32) for z in range(zlocal)]
    for k in range(views):
        smooth = [
            main[(k * zlocal + z) * both : (k * zlocal + z + 1) * both]
            + side[z][k * both : (k + 1) * both]
            for z in range(zlocal)
        ]
        at = (me ^ shifts[k]) * zlocal
        for f in range(2):
            parts = []
            for z in range(0, zlocal, 2):
                parts += split_stack(
                    jnp.concatenate(
                        [p[:, f * LANES : (f + 1) * LANES] for p in smooth[z : z + 2]], axis=1
                    )
                )
            operand = jnp.concatenate(parts, axis=0)
            out = jnp.dot(wy_ref[f], operand, preferred_element_type=F32)
            for z in range(zlocal):
                row, lane = z // 2 * both, z % 2 * LANES
                out_ref[f, at + z] = out[row : row + both, lane : lane + LANES]


def filter_kernel(chips, fields_ref, border_ref, column_ref, fields, dog_hbm, *refs):
    del fields_ref
    chosen, (dog_ref, written) = refs[: len(chips)], refs[len(chips) :]
    planes_z, rows = dog_ref.shape[:2]
    for f in range(2):
        fields[f, :, :RADIUS] += border_ref[f, :, :RADIUS]
        fields[f, :, rows - RADIUS :] += border_ref[f, :, RADIUS:]

    def tile(step, carry):
        at = pl.ds(pl.multiple_of(step * TILE, TILE), TILE)
        done = z_pass(lambda f, z: fields[f, z, at, :], planes_z)
        for z in range(planes_z):
            dog_ref[z, at, :] = done[z].astype(BF16)
        return carry

    lax.fori_loop(0, rows // TILE, tile, 0)

    parts = written.shape[0]
    copies = []
    for part in range(parts):
        span = pl.ds(part * (planes_z // parts), planes_z // parts)
        copies.append(
            pltpu.make_async_copy(dog_ref.at[span], dog_hbm.at[span], written.at[part])
        )
        copies[-1].start()

    half = planes_z * rows // 2
    flat = dog_ref[...].reshape(2 * half, LANES)
    flat = jnp.concatenate([flat[:half], flat[half:]], axis=1)
    columns = column_ref[...]
    offered = columns.shape[0]
    lane = lax.broadcasted_iota(jnp.int32, (offered, BLOCK), 1).astype(F32).astype(BF16)
    for m in range(2 * len(chips)):
        column = columns[:, m : m + 1]
        later = column >= half
        column = jnp.where(later, column - half, column)
        upper = jnp.floor(column * (1.0 / BLOCK))
        lower = column - BLOCK * upper
        onehot = []
        for j in range(half // BLOCK):
            here = jnp.where(upper == j, lower, -1.0).astype(BF16)
            onehot.append(jnp.where(lane == here, 1.0, 0.0).astype(BF16))
        onehot = jnp.concatenate(onehot, axis=1)
        picked = jnp.dot(onehot, flat, preferred_element_type=F32)
        picked = jnp.where(later, picked[:, LANES:], picked[:, :LANES])
        chosen[m // 2][m % 2] = picked.astype(BF16)
    for copy in copies:
        copy.wait()


def forward_kernel(target_ref, *refs):
    *rows, out_ref, _ = refs
    del target_ref
    for c, row in enumerate(rows):
        out_ref[c] = row[1]


def merge_rows(chips, core, rows, target_ref, slots, emit):
    owner = lax.axis_index("bulk")
    target = jnp.concatenate(
        [target_ref[pl.ds(partner(owner ^ core, c, 0), 1), :] for c in chips], axis=1
    )
    received = jnp.concatenate(rows, axis=0)
    upper, lower = target >> 8, (target & (BLOCK - 1)).astype(F32)
    place = lax.broadcasted_iota(jnp.int32, (BLOCK, target.shape[1]), 0).astype(F32).astype(BF16)
    for block in range(slots // BLOCK):
        wanted = jnp.where(upper == block, lower, -1.0).astype(BF16)
        onehot = jnp.where(place == wanted, 1.0, 0.0).astype(BF16)
        emit(block, jnp.dot(onehot, received, preferred_element_type=F32))


def merge_kernel(chips, target_ref, *refs):
    *rows, out_ref = refs

    def emit(block, sums):
        out_ref[block * BLOCK : (block + 1) * BLOCK] = sums

    merge_rows(chips, 0, [r[0] for r in rows], target_ref, out_ref.shape[0], emit)


def finish_kernel(chips, passed_ref, target_ref, sums_ref, out_hbm, out_ref, written):
    slots = out_ref.shape[0]
    copies = []

    def emit(block, sums):
        span = pl.ds(block * BLOCK, BLOCK)
        summed = sums_ref[span] + sums
        scale = lax.rsqrt(jnp.mean(summed * summed, axis=-1, keepdims=True) + epsilon)
        out_ref[span] = summed * scale
        copies.append(
            pltpu.make_async_copy(out_ref.at[span], out_hbm.at[span], written.at[block])
        )
        copies[-1].start()

    rows = [passed_ref[c] for c in range(len(chips))]
    merge_rows(chips, 1, rows, target_ref, slots, emit)
    for copy in copies:
        copy.wait()


def swap(block, axis, distance):
    if distance == 0:
        return block
    count = lax.axis_size(axis)
    return lax.ppermute(block, axis, [(i, i ^ distance) for i in range(count)])


def local(planes, cand_index, recv_slot, recv_count):
    views = lax.axis_size("view")
    bricks = lax.axis_size("bulk")
    zlocal, rows, width = planes.shape
    planes_z = zlocal * views
    owners, offered = cand_index.shape[2:]
    vmem = pl.BlockSpec(memory_space=pltpu.VMEM)
    hbm = pl.BlockSpec(memory_space=pltpu.HBM)
    params = pltpu.CompilerParams(vmem_limit_bytes=20 * 1024 * 1024)
    edge = jax.ShapeDtypeStruct((2, edge_rows(zlocal), LANES), BF16)
    body = jax.ShapeDtypeStruct((zlocal + 1, rows - 2 * RADIUS, LANES), BF16)
    halo = jax.ShapeDtypeStruct((views, edge_rows(zlocal), LANES), BF16)
    targets = jax.ShapeDtypeStruct((owners, offered), jnp.int32)
    shifts = list(range(views - 1, -1, -1))
    chips = list(range(owners - 2, -1, -2))
    chips = list(zip(chips, chips[:1] + chips[-2:0:-1] + chips[-1:]))

    packed = pl.pallas_call(
        lambda *refs: pack_kernel(shifts, *refs),
        out_shape=[edge] * views + [body] * views,
        in_specs=[vmem],
        out_specs=[vmem] * (2 * views),
        compiler_params=params,
    )(planes)
    edges = {k: swap(e, "view", k) for e, k in zip(packed[:views], shifts)}
    inner = {k: swap(e, "view", k) for e, k in zip(packed[views:], shifts)}
    edge_order = [2, 3, 1, 0] if views == 4 else shifts
    inner_order = [2, 3, 1] if views == 4 else shifts[:-1]

    pairs = zlocal // 2
    main_w, side_w, inside_w, margin_w = pl.pallas_call(
        prepare_kernel,
        out_shape=[
            jax.ShapeDtypeStruct((2 * LANES, 2 * LANES), BF16),
            jax.ShapeDtypeStruct((zlocal, 2 * LANES, 2 * LANES), BF16),
            jax.ShapeDtypeStruct((2, rows, 4 * rows), BF16),
            jax.ShapeDtypeStruct((2, 2 * RADIUS * pairs, 8 * RADIUS * pairs), BF16),
        ],
        in_specs=[vmem],
        out_specs=[vmem] * 4,
        compiler_params=params,
    )(edges[0])
    token = jax.ShapeDtypeStruct((RADIUS, LANES), F32)
    near, far, passed = pl.pallas_call(
        margin_kernel,
        out_shape=[halo] * 2 + [token],
        in_specs=[vmem] * views,
        out_specs=[vmem] * 3,
        compiler_params=params,
    )(*[edges[k] for k in edge_order])
    own, passed = pl.pallas_call(
        early_kernel,
        out_shape=[jax.ShapeDtypeStruct((2, zlocal, rows, LANES), F32), token],
        in_specs=[vmem] * 6,
        out_specs=[vmem] * 2,
        input_output_aliases={0: 1},
        compiler_params=params,
    )(passed, edges[0], inner[0], main_w, side_w, inside_w)
    columns, target = pl.pallas_call(
        lambda *refs: lists_kernel(chips, *refs),
        out_shape=[jax.ShapeDtypeStruct((offered, owners), F32), targets],
        in_specs=[vmem] * 4,
        out_specs=[vmem] * 2,
        compiler_params=params,
    )(
        passed,
        cand_index.reshape(owners, offered),
        recv_slot.reshape(owners, offered),
        recv_count.reshape(1, owners),
    )
    far_pairs = [(i, i + 1) for i in range(1, bricks - 1, 2)] + [(0, bricks - 1)]
    far_pairs = far_pairs + [(target, source) for source, target in far_pairs]
    far = lax.ppermute(far, "bulk", far_pairs)
    near = swap(near, "bulk", 1)

    whole = jax.ShapeDtypeStruct((2, planes_z, rows, LANES), F32)
    fields, target = pl.pallas_call(
        lambda *refs: late_kernel(inner_order, *refs),
        out_shape=[whole, targets],
        in_specs=[vmem] * (2 * views + 3),
        out_specs=[vmem] * 2,
        input_output_aliases={0: 1},
        compiler_params=params,
    )(
        target,
        own,
        *[edges[k] for k in inner_order],
        *[inner[k] for k in inner_order],
        main_w,
        side_w,
        inside_w,
    )
    border, target = pl.pallas_call(
        lambda *refs: border_kernel(edge_order, *refs),
        out_shape=[jax.ShapeDtypeStruct((2, planes_z, 2 * RADIUS, LANES), F32), targets],
        in_specs=[vmem] * 6,
        out_specs=[vmem] * 2,
        input_output_aliases={0: 1},
        compiler_params=params,
    )(target, near, far, main_w, side_w, margin_w)

    offers = jax.ShapeDtypeStruct((2, offered, LANES), BF16)
    _, dog, *chosen = pl.pallas_call(
        lambda *refs: filter_kernel(chips, *refs),
        out_shape=[whole, jax.ShapeDtypeStruct((planes_z, rows, LANES), BF16)]
        + [offers] * len(chips),
        in_specs=[vmem] * 3,
        out_specs=[vmem, hbm] + [vmem] * len(chips),
        input_output_aliases={0: 0},
        scratch_shapes=[
            pltpu.VMEM((planes_z, rows, LANES), BF16),
            pltpu.SemaphoreType.DMA((8,)),
        ],
        compiler_params=params,
    )(fields, border, columns)
    received = [
        lax.ppermute(c, "bulk", [(i, i ^ chip[i % 2]) for i in range(bricks)]) if max(chip) else c
        for c, chip in zip(chosen, chips)
    ]
    passed, target = pl.pallas_call(
        forward_kernel,
        out_shape=[jax.ShapeDtypeStruct((len(chips), offered, LANES), BF16), targets],
        in_specs=[vmem] * (len(chips) + 1),
        out_specs=[vmem] * 2,
        input_output_aliases={0: 1},
        compiler_params=params,
    )(target, *received)
    passed = swap(passed, "bulk", 1)
    sums = pl.pallas_call(
        lambda *refs: merge_kernel(chips, *refs),
        out_shape=jax.ShapeDtypeStruct((SLOTS, LANES), F32),
        in_specs=[vmem] * (len(chips) + 1),
        out_specs=vmem,
        compiler_params=params,
    )(target, *received)
    descriptors = pl.pallas_call(
        lambda *refs: finish_kernel(chips, *refs),
        out_shape=jax.ShapeDtypeStruct((SLOTS, LANES), F32),
        in_specs=[vmem] * 3,
        out_specs=hbm,
        scratch_shapes=[
            pltpu.VMEM((SLOTS, LANES), F32),
            pltpu.SemaphoreType.DMA((SLOTS // BLOCK,)),
        ],
        compiler_params=params,
    )(passed, target, sums)
    return (dog, descriptors.reshape(1, 1, SLOTS, LANES))


def solution(mesh):
    in_specs = (
        P("view", "bulk", None),
        P("bulk", "view", None, None),
        P("bulk", "view", None, None),
        P("bulk", "view", None),
    )
    out_specs = (P(None, "bulk", "view"), P("bulk", "view", None, None))
    return jax.shard_map(local, mesh=mesh, in_specs=in_specs, out_specs=out_specs, check_vma=False)
```

```python
import math

import jax
import jax.numpy as jnp
import numpy as np
from jax import lax
from jax.experimental import pallas as pl
from jax.experimental.pallas import tpu as pltpu
from jax.sharding import PartitionSpec as P

RADIUS = 8
SLOTS = 1024
LANES = 128
BLOCK = 256
TILE = 16

narrow_sigma = (1.0, 2.0, 2.0)
broad_sigma = (1.6, 3.2, 3.2)
contrast = 20.0
epsilon = 1e-06

F32 = jnp.float32
BF16 = jnp.bfloat16


def gauss_taps(sigma, radius):
    weights = [math.exp(-0.5 * (offset / sigma) ** 2) for offset in range(-radius, radius + 1)]
    scale_total = sum(weights)
    return [weight / scale_total for weight in weights]


def taps(along):
    return [
        np.asarray(gauss_taps(sigma[along], RADIUS), np.float32)
        for sigma in (narrow_sigma, broad_sigma)
    ]


def stencil(distance, tap):
    total = jnp.zeros(distance.shape, F32)
    for reach in range(RADIUS + 1):
        total = jnp.where(jnp.abs(distance) == reach, float(tap[RADIUS + reach]), total)
    return total


def split(weight):
    high = weight.astype(BF16).astype(F32)
    return high, (weight - high).astype(BF16).astype(F32)


def grid(rows, columns):
    shape = (rows, columns)
    return [lax.broadcasted_iota(jnp.int32, shape, axis) for axis in range(2)]


def x_weights(wm_ref, ws_ref):
    row, column = grid(LANES, LANES)
    place = row % (2 * RADIUS)
    margin = jnp.where(place < RADIUS, place - RADIUS, place - RADIUS + LANES)
    group = lax.broadcasted_iota(jnp.int32, (LANES, 2 * LANES), 0) // (2 * RADIUS)
    for ref, at in ((wm_ref, row), (ws_ref, margin)):
        whole = jnp.concatenate([stencil(at - column, tap) for tap in taps(2)], axis=1)
        for part, value in enumerate(split(whole)):
            span = slice(part * LANES, (part + 1) * LANES)
            if ref is wm_ref:
                ref[span] = value.astype(BF16)
                continue
            for z in range(ref.shape[0]):
                ref[z, span] = jnp.where(group == z, value, 0.0).astype(BF16)


def y_weights(odd, out_ref):
    rows = out_ref.shape[1]
    out, lane = grid(rows, 4 * rows)
    place, block = lane % rows, lane // rows
    first = jnp.where(odd, place, place + rows - RADIUS)
    second = jnp.where(odd, place + rows - 2 * RADIUS, place - RADIUS)
    at = jnp.where(place < RADIUS, first, jnp.where(place < 2 * RADIUS, second, place - RADIUS))
    for f, tap in enumerate(taps(1)):
        high, low = split(stencil(at - out, tap))
        out_ref[f] = jnp.where(block % 2 == 0, high, low).astype(BF16)


def y_margin_weights(odd, rows, out_ref):
    both = 2 * RADIUS
    row, lane = grid(*out_ref.shape[1:])
    out = row % both
    out = jnp.where(out < RADIUS, out, out + rows - both)
    block, place = lane % (4 * both) // both, lane % both
    low, high = place % RADIUS - RADIUS, place % RADIUS + rows
    near = place < RADIUS
    at = jnp.where(jnp.logical_xor(near, odd), high, low)
    same = row // both == lane // (4 * both)
    for f, tap in enumerate(taps(1)):
        top, rest = split(stencil(at - out, tap))
        value = jnp.where(block % 2 == 0, top, rest)
        out_ref[f] = jnp.where(same, value, 0.0).astype(BF16)


def edge_rows(zlocal):
    return -(-(zlocal + 1) * RADIUS // 16) * 16


def column_tile(source, which):
    at = pl.ds(pl.multiple_of(which * LANES, LANES), LANES)
    return source(at)


def with_margin(source, dest, views, rows):
    lane = lax.broadcasted_iota(jnp.int32, (rows, LANES), 1)
    left = column_tile(source, jnp.maximum(dest - 1, 0))
    right = column_tile(source, jnp.minimum(dest + 1, views - 1))
    lowest = jnp.where(dest > 0, LANES - RADIUS, LANES)
    highest = jnp.where(dest < views - 1, RADIUS, 0)
    margin = jnp.where(lane < highest, right, jnp.where(lane >= lowest, left, 0.0))
    return column_tile(source, dest), margin


def place_margin(margin, z):
    return pltpu.roll(margin, (2 * RADIUS * z + RADIUS) % LANES, 1)


def pack_kernel(shifts, planes_ref, *outs):
    views = len(shifts)
    edges, inner = outs[:views], outs[views:]
    zlocal, rows = planes_ref.shape[:2]
    me = lax.axis_index("view")
    odd = lax.axis_index("bulk") % 2 == 1
    for k, shift in enumerate(shifts):
        groups = []
        packed = None
        for z in range(zlocal):
            main, margin = with_margin(
                lambda at: planes_ref[z, :, at].astype(F32), me ^ shift, views, rows
            )
            groups.append(main)
            placed = place_margin(margin, z)
            packed = placed if packed is None else packed + placed
        groups.append(packed)
        low = [g[:RADIUS] for g in groups]
        high = [g[rows - RADIUS :] for g in groups]
        pad = edges[k].shape[1] - len(groups) * RADIUS
        if pad:
            low.append(jnp.zeros((pad, LANES), F32))
            high.append(jnp.zeros((pad, LANES), F32))
        low, high = jnp.concatenate(low, axis=0), jnp.concatenate(high, axis=0)
        edges[k][0] = jnp.where(odd, low, high).astype(BF16)
        edges[k][1] = jnp.where(odd, high, low).astype(BF16)
        for g, group in enumerate(groups):
            inner[k][g] = group[RADIUS : rows - RADIUS].astype(BF16)


def margin_kernel(*refs):
    *edges, near_ref, far_ref, token_ref = refs
    token_ref[...] = jnp.zeros(token_ref.shape, F32)
    for k, edge in enumerate(edges):
        near_ref[k] = edge[0]
        far_ref[k] = edge[1]


def partner(brick, chip, core):
    return brick ^ jnp.where(brick % 2 == 1, chip[1], chip[0]) ^ core


def prepare_kernel(packed_ref, wm_ref, ws_ref, inside_ref, margin_ref):
    del packed_ref
    odd = lax.axis_index("bulk") % 2 == 1
    x_weights(wm_ref, ws_ref)
    y_weights(odd, inside_ref)
    y_margin_weights(odd, inside_ref.shape[1], margin_ref)


def lists_kernel(chips, token_ref, index_ref, slot_ref, count_ref, column_ref, target_ref):
    del token_ref
    brick = lax.axis_index("bulk")
    wanted = jnp.concatenate(
        [index_ref[pl.ds(partner(brick, c, core), 1), :] for c in chips for core in range(2)],
        axis=0,
    )
    column_ref[...] = jnp.transpose(wanted.astype(F32))
    candidate = lax.broadcasted_iota(jnp.int32, slot_ref.shape, 1)
    counts = jnp.broadcast_to(count_ref[...].astype(F32), (LANES, count_ref.shape[1]))
    counts = jnp.transpose(counts)[:, : slot_ref.shape[1]].astype(jnp.int32)
    target_ref[...] = jnp.where(candidate < counts, slot_ref[...], -1)


def twice(block):
    return jnp.concatenate([block, block], axis=1)


def split_stack(data):
    high = data.astype(BF16)
    low = (data - high.astype(F32)).astype(BF16)
    return [high, high, low, low]


def z_pass(load, planes_z):
    data = [[load(f, z) for z in range(planes_z)] for f in range(2)]
    z_taps = taps(0)
    scale = (contrast, -contrast)
    out = []
    for z in range(planes_z):
        total = None
        for f in range(2):
            for reach in range(RADIUS + 1):
                weight = float(scale[f] * z_taps[f][RADIUS + reach])
                near = [z] if reach == 0 else [z - reach, z + reach]
                sides = [data[f][q] for q in near if 0 <= q < planes_z]
                if not sides:
                    continue
                both = sides[0] if len(sides) == 1 else sides[0] + sides[1]
                term = weight * both
                total = term if total is None else total + term
        out.append(total)
    return out


def plane_passes(edges, inner, wm_ref, ws_ref, wy_ref, write):
    count = len(edges)
    zlocal, rows = inner[0].shape[0] - 1, wy_ref.shape[1]
    small = [[e[part].astype(F32) for part in range(2)] for e in edges]

    def rows_of(k, g):
        top = [s[g * RADIUS : (g + 1) * RADIUS] for s in small[k]]
        return [jnp.concatenate(top, axis=0).astype(BF16), inner[k][g]]

    def stacked(z):
        return twice(jnp.concatenate([p for k in range(count) for p in rows_of(k, z)], axis=0))

    margins = stacked(zlocal)

    def x_pass(z):
        main = jnp.dot(stacked(z), wm_ref[...], preferred_element_type=F32)
        return main + jnp.dot(margins, ws_ref[z], preferred_element_type=F32)

    for z in range(0, zlocal, 2):
        pair = [x_pass(z), x_pass(z + 1)]
        for k in range(count):
            for f in range(2):
                data = jnp.concatenate(
                    [
                        p[k * rows : (k + 1) * rows, f * LANES : (f + 1) * LANES]
                        for p in pair
                    ],
                    axis=1,
                )
                operand = jnp.concatenate(split_stack(data), axis=0)
                out = jnp.dot(wy_ref[f], operand, preferred_element_type=F32)
                write(k, z, f, out[:, :LANES])
                write(k, z + 1, f, out[:, LANES:])


def early_kernel(token_ref, edge_ref, inner_ref, wm_ref, ws_ref, wy_ref, out_ref, _):
    del token_ref

    def write(k, z, f, value):
        del k
        out_ref[f, z] = value

    plane_passes([edge_ref], [inner_ref], wm_ref, ws_ref, wy_ref, write)


def late_kernel(shifts, target_ref, own_ref, *refs):
    del target_ref
    *refs, wm_ref, ws_ref, wy_ref, fields, _ = refs
    count = len(refs) // 2
    zlocal = own_ref.shape[1]
    me = lax.axis_index("view")
    for f in range(2):
        fields[f, pl.ds(me * zlocal, zlocal)] = own_ref[f]

    def write(k, z, f, value):
        fields[f, (me ^ shifts[k]) * zlocal + z] = value

    plane_passes(refs[:count], refs[count:], wm_ref, ws_ref, wy_ref, write)


def border_kernel(shifts, target_ref, near_ref, far_ref, wm_ref, ws_ref, wy_ref, out_ref, _):
    del target_ref
    views = len(shifts)
    halo = (near_ref, far_ref)
    zlocal = out_ref.shape[1] // views
    both = 2 * RADIUS
    me = lax.axis_index("view")
    brick = lax.axis_index("bulk")
    ends = (brick == 0) | (brick == lax.axis_size("bulk") - 1)

    def margin(part, k):
        data = halo[part][k].astype(F32)
        return jnp.where(ends, 0.0, data) if part == 1 else data

    small = [[margin(part, k) for part in range(2)] for k in range(views)]

    def rows_of(k, g):
        return [s[g * RADIUS : (g + 1) * RADIUS] for s in small[k]]

    main = [p for k in range(views) for z in range(zlocal) for p in rows_of(k, z)]
    side = [p for k in range(views) for p in rows_of(k, zlocal)]
    main = twice(jnp.concatenate(main, axis=0).astype(BF16))
    side = twice(jnp.concatenate(side, axis=0).astype(BF16))
    main = jnp.dot(main, wm_ref[...], preferred_element_type=F32)
    side = [jnp.dot(side, ws_ref[z], preferred_element_type=F32) for z in range(zlocal)]
    for k in range(views):
        smooth = [
            main[(k * zlocal + z) * both : (k * zlocal + z + 1) * both]
            + side[z][k * both : (k + 1) * both]
            for z in range(zlocal)
        ]
        at = (me ^ shifts[k]) * zlocal
        for f in range(2):
            parts = []
            for z in range(0, zlocal, 2):
                parts += split_stack(
                    jnp.concatenate(
                        [p[:, f * LANES : (f + 1) * LANES] for p in smooth[z : z + 2]], axis=1
                    )
                )
            operand = jnp.concatenate(parts, axis=0)
            out = jnp.dot(wy_ref[f], operand, preferred_element_type=F32)
            for z in range(zlocal):
                row, lane = z // 2 * both, z % 2 * LANES
                out_ref[f, at + z] = out[row : row + both, lane : lane + LANES]


def filter_kernel(chips, fields_ref, border_ref, column_ref, fields, dog_hbm, *refs):
    del fields_ref
    chosen, (dog_ref, written) = refs[: len(chips)], refs[len(chips) :]
    planes_z, rows = dog_ref.shape[:2]
    for f in range(2):
        fields[f, :, :RADIUS] += border_ref[f, :, :RADIUS]
        fields[f, :, rows - RADIUS :] += border_ref[f, :, RADIUS:]

    def tile(step, carry):
        at = pl.ds(pl.multiple_of(step * TILE, TILE), TILE)
        done = z_pass(lambda f, z: fields[f, z, at, :], planes_z)
        for z in range(planes_z):
            dog_ref[z, at, :] = done[z].astype(BF16)
        return carry

    lax.fori_loop(0, rows // TILE, tile, 0)

    parts = written.shape[0]
    copies = []
    for part in range(parts):
        span = pl.ds(part * (planes_z // parts), planes_z // parts)
        copies.append(
            pltpu.make_async_copy(dog_ref.at[span], dog_hbm.at[span], written.at[part])
        )
        copies[-1].start()

    half = planes_z * rows // 2
    flat = dog_ref[...].reshape(2 * half, LANES)
    flat = jnp.concatenate([flat[:half], flat[half:]], axis=1)
    columns = column_ref[...]
    offered = columns.shape[0]
    lane = lax.broadcasted_iota(jnp.int32, (offered, BLOCK), 1).astype(F32).astype(BF16)
    for m in range(2 * len(chips)):
        column = columns[:, m : m + 1]
        later = column >= half
        column = jnp.where(later, column - half, column)
        upper = jnp.floor(column * (1.0 / BLOCK))
        lower = column - BLOCK * upper
        onehot = []
        for j in range(half // BLOCK):
            here = jnp.where(upper == j, lower, -1.0).astype(BF16)
            onehot.append(jnp.where(lane == here, 1.0, 0.0).astype(BF16))
        onehot = jnp.concatenate(onehot, axis=1)
        picked = jnp.dot(onehot, flat, preferred_element_type=F32)
        picked = jnp.where(later, picked[:, LANES:], picked[:, :LANES])
        chosen[m // 2][m % 2] = picked.astype(BF16)
    for copy in copies:
        copy.wait()


def forward_kernel(target_ref, *refs):
    *rows, out_ref, _ = refs
    del target_ref
    for c, row in enumerate(rows):
        out_ref[c] = row[1]


def merge_rows(chips, core, rows, target_ref, slots, emit):
    owner = lax.axis_index("bulk")
    target = jnp.concatenate(
        [target_ref[pl.ds(partner(owner ^ core, c, 0), 1), :] for c in chips], axis=1
    )
    received = jnp.concatenate(rows, axis=0)
    upper, lower = target >> 8, (target & (BLOCK - 1)).astype(F32)
    place = lax.broadcasted_iota(jnp.int32, (BLOCK, target.shape[1]), 0).astype(F32).astype(BF16)
    for block in range(slots // BLOCK):
        wanted = jnp.where(upper == block, lower, -1.0).astype(BF16)
        onehot = jnp.where(place == wanted, 1.0, 0.0).astype(BF16)
        emit(block, jnp.dot(onehot, received, preferred_element_type=F32))


def merge_kernel(chips, target_ref, *refs):
    *rows, out_ref = refs

    def emit(block, sums):
        out_ref[block * BLOCK : (block + 1) * BLOCK] = sums

    merge_rows(chips, 0, [r[0] for r in rows], target_ref, out_ref.shape[0], emit)


def finish_kernel(chips, passed_ref, target_ref, sums_ref, out_hbm, out_ref, written):
    slots = out_ref.shape[0]
    copies = []

    def emit(block, sums):
        span = pl.ds(block * BLOCK, BLOCK)
        summed = sums_ref[span] + sums
        scale = lax.rsqrt(jnp.mean(summed * summed, axis=-1, keepdims=True) + epsilon)
        out_ref[span] = summed * scale
        copies.append(
            pltpu.make_async_copy(out_ref.at[span], out_hbm.at[span], written.at[block])
        )
        copies[-1].start()

    rows = [passed_ref[c] for c in range(len(chips))]
    merge_rows(chips, 1, rows, target_ref, slots, emit)
    for copy in copies:
        copy.wait()


def swap(block, axis, distance):
    if distance == 0:
        return block
    count = lax.axis_size(axis)
    return lax.ppermute(block, axis, [(i, i ^ distance) for i in range(count)])


def local(planes, cand_index, recv_slot, recv_count):
    views = lax.axis_size("view")
    bricks = lax.axis_size("bulk")
    zlocal, rows, width = planes.shape
    planes_z = zlocal * views
    owners, offered = cand_index.shape[2:]
    vmem = pl.BlockSpec(memory_space=pltpu.VMEM)
    hbm = pl.BlockSpec(memory_space=pltpu.HBM)
    params = pltpu.CompilerParams(vmem_limit_bytes=20 * 1024 * 1024)
    edge = jax.ShapeDtypeStruct((2, edge_rows(zlocal), LANES), BF16)
    body = jax.ShapeDtypeStruct((zlocal + 1, rows - 2 * RADIUS, LANES), BF16)
    halo = jax.ShapeDtypeStruct((views, edge_rows(zlocal), LANES), BF16)
    targets = jax.ShapeDtypeStruct((owners, offered), jnp.int32)
    shifts = list(range(views - 1, -1, -1))
    chips = list(range(owners - 2, -1, -2))
    chips = list(zip(chips, chips[:1] + chips[-2:0:-1] + chips[-1:]))

    packed = pl.pallas_call(
        lambda *refs: pack_kernel(shifts, *refs),
        out_shape=[edge] * views + [body] * views,
        in_specs=[vmem],
        out_specs=[vmem] * (2 * views),
        compiler_params=params,
    )(planes)
    edges = {k: swap(e, "view", k) for e, k in zip(packed[:views], shifts)}
    inner = {k: swap(e, "view", k) for e, k in zip(packed[views:], shifts)}
    edge_order = [2, 3, 1, 0] if views == 4 else shifts
    inner_order = [2, 3, 1] if views == 4 else shifts[:-1]

    pairs = zlocal // 2
    main_w, side_w, inside_w, margin_w = pl.pallas_call(
        prepare_kernel,
        out_shape=[
            jax.ShapeDtypeStruct((2 * LANES, 2 * LANES), BF16),
            jax.ShapeDtypeStruct((zlocal, 2 * LANES, 2 * LANES), BF16),
            jax.ShapeDtypeStruct((2, rows, 4 * rows), BF16),
            jax.ShapeDtypeStruct((2, 2 * RADIUS * pairs, 8 * RADIUS * pairs), BF16),
        ],
        in_specs=[vmem],
        out_specs=[vmem] * 4,
        compiler_params=params,
    )(edges[0])
    token = jax.ShapeDtypeStruct((RADIUS, LANES), F32)
    near, far, passed = pl.pallas_call(
        margin_kernel,
        out_shape=[halo] * 2 + [token],
        in_specs=[vmem] * views,
        out_specs=[vmem] * 3,
        compiler_params=params,
    )(*[edges[k] for k in edge_order])
    own, passed = pl.pallas_call(
        early_kernel,
        out_shape=[jax.ShapeDtypeStruct((2, zlocal, rows, LANES), F32), token],
        in_specs=[vmem] * 6,
        out_specs=[vmem] * 2,
        input_output_aliases={0: 1},
        compiler_params=params,
    )(passed, edges[0], inner[0], main_w, side_w, inside_w)
    columns, target = pl.pallas_call(
        lambda *refs: lists_kernel(chips, *refs),
        out_shape=[jax.ShapeDtypeStruct((offered, owners), F32), targets],
        in_specs=[vmem] * 4,
        out_specs=[vmem] * 2,
        compiler_params=params,
    )(
        passed,
        cand_index.reshape(owners, offered),
        recv_slot.reshape(owners, offered),
        recv_count.reshape(1, owners),
    )
    far_pairs = [(i, i + 1) for i in range(1, bricks - 1, 2)] + [(0, bricks - 1)]
    far_pairs = far_pairs + [(target, source) for source, target in far_pairs]
    far = lax.ppermute(far, "bulk", far_pairs)
    near = swap(near, "bulk", 1)

    whole = jax.ShapeDtypeStruct((2, planes_z, rows, LANES), F32)
    border, target = pl.pallas_call(
        lambda *refs: border_kernel(edge_order, *refs),
        out_shape=[jax.ShapeDtypeStruct((2, planes_z, 2 * RADIUS, LANES), F32), targets],
        in_specs=[vmem] * 6,
        out_specs=[vmem] * 2,
        input_output_aliases={0: 1},
        compiler_params=params,
    )(target, near, far, main_w, side_w, margin_w)
    fields, target = pl.pallas_call(
        lambda *refs: late_kernel(inner_order, *refs),
        out_shape=[whole, targets],
        in_specs=[vmem] * (2 * views + 3),
        out_specs=[vmem] * 2,
        input_output_aliases={0: 1},
        compiler_params=params,
    )(
        target,
        own,
        *[edges[k] for k in inner_order],
        *[inner[k] for k in inner_order],
        main_w,
        side_w,
        inside_w,
    )
    offers = jax.ShapeDtypeStruct((2, offered, LANES), BF16)
    _, dog, *chosen = pl.pallas_call(
        lambda *refs: filter_kernel(chips, *refs),
        out_shape=[whole, jax.ShapeDtypeStruct((planes_z, rows, LANES), BF16)]
        + [offers] * len(chips),
        in_specs=[vmem] * 3,
        out_specs=[vmem, hbm] + [vmem] * len(chips),
        input_output_aliases={0: 0},
        scratch_shapes=[
            pltpu.VMEM((planes_z, rows, LANES), BF16),
            pltpu.SemaphoreType.DMA((8,)),
        ],
        compiler_params=params,
    )(fields, border, columns)
    received = [
        lax.ppermute(c, "bulk", [(i, i ^ chip[i % 2]) for i in range(bricks)]) if max(chip) else c
        for c, chip in zip(chosen, chips)
    ]
    passed, target = pl.pallas_call(
        forward_kernel,
        out_shape=[jax.ShapeDtypeStruct((len(chips), offered, LANES), BF16), targets],
        in_specs=[vmem] * (len(chips) + 1),
        out_specs=[vmem] * 2,
        input_output_aliases={0: 1},
        compiler_params=params,
    )(target, *received)
    passed = swap(passed, "bulk", 1)
    sums = pl.pallas_call(
        lambda *refs: merge_kernel(chips, *refs),
        out_shape=jax.ShapeDtypeStruct((SLOTS, LANES), F32),
        in_specs=[vmem] * (len(chips) + 1),
        out_specs=vmem,
        compiler_params=params,
    )(target, *received)
    descriptors = pl.pallas_call(
        lambda *refs: finish_kernel(chips, *refs),
        out_shape=jax.ShapeDtypeStruct((SLOTS, LANES), F32),
        in_specs=[vmem] * 3,
        out_specs=hbm,
        scratch_shapes=[
            pltpu.VMEM((SLOTS, LANES), F32),
            pltpu.SemaphoreType.DMA((SLOTS // BLOCK,)),
        ],
        compiler_params=params,
    )(passed, target, sums)
    return (dog, descriptors.reshape(1, 1, SLOTS, LANES))


def solution(mesh):
    in_specs = (
        P("view", "bulk", None),
        P("bulk", "view", None, None),
        P("bulk", "view", None, None),
        P("bulk", "view", None),
    )
    out_specs = (P(None, "bulk", "view"), P("bulk", "view", None, None))
    return jax.shard_map(local, mesh=mesh, in_specs=in_specs, out_specs=out_specs, check_vma=False)
```
